768 devices in a mesh: section: 24 (over z, y_hi), dp: 32 (over x, y_lo, core).
Axes of the slice: x: 4, y: 8 (y_hi: 2, y_lo: 4; y = y_hi * 4 + y_lo), z: 12, core: 2. Of those that a mesh axis runs over, the one named last changes fastest.
Arguments:
- feed_down: bfloat16 [24, 2048, 4096], P('section', 'dp'), may hold values from -6 to 6
- feed_up: bfloat16 [24, 2048, 4096], P('section', 'dp'), may hold values from -6 to 6
- cotangent_down: bfloat16 [24, 2048, 4096], P('section', 'dp'), may hold values from -6 to 6
- cotangent_up: bfloat16 [24, 2048, 4096], P('section', 'dp'), may hold values from -6 to 6
- roster: int32 [24, 2, 2], P('section'), may hold values from 0 to 1, each once within a row
- value_weight: bfloat16 [24, 4096, 512], P('section'), may hold values from -0.09375 to 0.09375
Outputs:
- next_down: bfloat16 [24, 2048, 4096], P('section', 'dp')
- next_up: bfloat16 [24, 2048, 4096], P('section', 'dp')
- back_down: bfloat16 [24, 2048, 4096], P('section', 'dp')
- back_up: bfloat16 [24, 2048, 4096], P('section', 'dp')
- grad_weight: float32 [24, 4096, 512], P('section', 'dp')
The draws below stay inside these ranges and needn't reach their ends.
Inputs may be any that keep to these rules, and one draw needn't show every extreme that they name: roster[s, 0, :] and roster[s, 1, :] are each a permutation of the 2 micro-batches: block j of the cotangents that section index s receives for a leg belongs to micro-batch roster[s, leg, j].
All inputs are finite; a program needn't handle non-finite values.
Results may differ from the reference program's by a relative error of at most 0.005.
Values may be sent and summed in bfloat16 or wider, within the bound.
A program may use at most 64 MiB of HBM per device.

```python
import jax
import jax.numpy as jnp
from jax import lax

D = 4096
KVH = 4
HD = 128
GROUPS = 8
MB = 2
RM = 32
TOKS = 2048
N_SECTION = 24
N_DP = 32


def steps_of(own_key, dims, split, smallest, largest):
    level, own = 1.0, jax.random.fold_in(own_key, 6)
    for axis_at, shards_of in split:
        steps = jnp.exp(jax.random.uniform(jax.random.fold_in(own, axis_at), (shards_of,), jnp.float32, smallest / len(split), largest / len(split)))
        level = level * jnp.repeat(steps, dims[axis_at] // shards_of).reshape([-1 if axis == axis_at else 1 for axis in range(len(dims))])
    return level


def bell_draw(rng, shape, scale, bound, split=(), held_as=jnp.bfloat16):
    gain = steps_of(rng, shape, split, -0.22, 0.18) if split else 1.0
    array = jax.random.normal(rng, shape, jnp.float32) * scale * gain
    return jnp.minimum(jnp.maximum(array, -bound), bound).astype(held_as)


def setup_inputs(seed: int = 0) -> dict:
    key_list = jax.random.split(jax.random.key(seed), 7)
    feed_down = bell_draw(key_list[0], (N_SECTION, TOKS, D), 1.0, 6.0, ((0, 24), (1, 32)))
    feed_up = bell_draw(key_list[1], (N_SECTION, TOKS, D), 1.0, 6.0, ((0, 24), (1, 32)))
    cotangent_down = bell_draw(key_list[2], (N_SECTION, TOKS, D), 1.0, 6.0, ((0, 24), (1, 32)))
    cotangent_up = bell_draw(key_list[3], (N_SECTION, TOKS, D), 1.0, 6.0, ((0, 24), (1, 32)))
    roster = jax.vmap(lambda own: jax.random.permutation(own, MB))(jax.random.split(key_list[4], N_SECTION * 2)).reshape((N_SECTION, 2, MB)).astype(jnp.int32)
    value_weight = bell_draw(key_list[5], (N_SECTION, D, KVH * HD), D ** -0.5, 0.09375, ((0, 24),))
    return dict(feed_down=feed_down, feed_up=feed_up, cotangent_down=cotangent_down, cotangent_up=cotangent_up, roster=roster, value_weight=value_weight)


EPSILON = 1e-05

def normalize(inputs):
    values = inputs.astype(jnp.float32)
    inverse = lax.rsqrt(lax.optimization_barrier(jnp.mean(values * values, axis=-1, keepdims=True)) + EPSILON)
    return (values * inverse, inverse)

def arrange(received, roster_row, devices):
    blocks = roster_row.shape[0]
    match_table = (roster_row[:, None] == jnp.arange(blocks, dtype=jnp.int32)[None, :]).astype(jnp.float32)
    shaped = received.reshape(devices, blocks, -1).astype(jnp.float32)
    placed = jnp.einsum('pjx,jm->pmx', shaped, match_table)
    return placed.astype(jnp.bfloat16).reshape(received.shape)

def one_leg(inputs, grads, weight):
    scaled, inverse = normalize(inputs)
    normed = scaled.astype(jnp.bfloat16)
    values = jnp.dot(normed, weight, preferred_element_type=jnp.float32)
    row_total = inputs.shape[0]
    spread = jnp.broadcast_to(values.reshape(row_total, KVH, 1, HD), (row_total, KVH, GROUPS, HD)).reshape(row_total, -1)
    advanced = (inputs.astype(jnp.float32) + spread).astype(jnp.bfloat16)
    grouped = lax.optimization_barrier(jnp.sum(grads.astype(jnp.float32).reshape(row_total, KVH, GROUPS, HD), axis=2)).reshape(row_total, -1).astype(jnp.bfloat16)
    back_norm = jnp.dot(grouped, weight.T, preferred_element_type=jnp.float32)
    through = inverse * (back_norm - scaled * lax.optimization_barrier(jnp.mean(back_norm * scaled, axis=-1, keepdims=True)))
    behind = (grads.astype(jnp.float32) + through).astype(jnp.bfloat16)
    return (advanced, behind, normed, grouped)

def reference(feed_down, feed_up, cotangent_down, cotangent_up, roster, value_weight):
    sections = feed_down.shape[0]
    factor = float(2 * MB * RM * N_DP) ** (-0.5)

    def per_section(section_index):
        lower_index = (section_index - 1) % sections
        upper_index = (section_index + 1) % sections
        weight = value_weight[section_index]
        grads_down = arrange(cotangent_down[upper_index], roster[section_index, 0], N_DP)
        grads_up = arrange(cotangent_up[lower_index], roster[section_index, 1], N_DP)
        advanced_down, behind_down, normed_down, grouped_down = one_leg(feed_down[lower_index], grads_down, weight)
        advanced_up, behind_up, normed_up, grouped_up = one_leg(feed_up[upper_index], grads_up, weight)
        normed_all = jnp.concatenate([normed_down, normed_up], axis=0)
        grouped_all = jnp.concatenate([grouped_down, grouped_up], axis=0)
        total = jnp.dot(normed_all.T, grouped_all, preferred_element_type=jnp.float32)
        return (advanced_down, advanced_up, behind_down, behind_up, total * factor)
    next_down, next_up, back_down, back_up, grad_weight = lax.map(per_section, jnp.arange(sections, dtype=jnp.int32))
    return (next_down, next_up, back_down, back_up, grad_weight)
```

```python
import jax
import jax.numpy as jnp
from jax import lax
from jax.experimental import pallas as pl
from jax.experimental.pallas import tpu as pltpu
from jax.sharding import PartitionSpec as P

MESH = pl.DeviceIdType.MESH
F32 = jnp.float32
BF16 = jnp.bfloat16

KVH = 4
HD = 128
GROUPS = 8
SPAN = GROUPS * HD
D = KVH * SPAN
NX, NY, NC = 4, 4, 2
ROWS = 64
BLOCK = 32
TOK = 2 * ROWS
EPSILON = 1e-05
EARLY = KVH - 1


def kernel(
    factor,
    feed_down,
    feed_up,
    cot_down,
    cot_up,
    roster,
    weight,
    next_down,
    next_up,
    back_down,
    back_up,
    grad,
    x_in,
    g_in,
    early_own,
    early_send,
    early_recv,
    w_buf,
    normed,
    turned,
    inverse,
    grouped,
    values,
    through,
    next_buf,
    back_buf,
    keep,
    core_send,
    core_recv,
    x_send,
    x_recv,
    x_total,
    y_send,
    y_recv,
    grad_buf,
    feed_ss,
    feed_rs,
    cot_ss,
    cot_rs,
    early_ss,
    early_rs,
    core_ss,
    core_rs,
    x_ss,
    x_rs,
    y_ss,
    y_rs,
    local_sem,
    out_sem,
):
    sections = lax.axis_size("section")
    s = lax.axis_index("section")
    d = lax.axis_index("dp")
    x = d // (NY * NC)
    y = (d // NC) % NY
    c = d % NC
    ahead = (lax.rem(s + 1, sections), d)
    behind = (lax.rem(s + sections - 1, sections), d)
    twin = (s, d + 1 - 2 * c)

    def x_peer(j):
        return (s, ((x + j) % NX) * (NY * NC) + y * NC + c)

    def y_peer(j):
        return (s, x * (NY * NC) + ((y + j) % NY) * NC + c)

    partners = [ahead, behind, twin]
    partners += [x_peer(j) for j in range(1, NX)]
    partners += [y_peer(j) for j in range(1, NY)]
    barrier = pltpu.get_barrier_semaphore()
    for partner in partners:
        pl.semaphore_signal(barrier, inc=1, device_id=partner, device_id_type=MESH)
    pl.semaphore_wait(barrier, len(partners))

    def remote(src, dst, ss, rs, to):
        return pltpu.make_async_remote_copy(
            src_ref=src, dst_ref=dst, send_sem=ss, recv_sem=rs, device_id=to, device_id_type=MESH
        )

    feeds, cots, earlies = [], [], []
    for h in range(2):
        rows = slice(h * BLOCK, (h + 1) * BLOCK)
        for leg, (src, to) in enumerate(((feed_down, ahead), (feed_up, behind))):
            feeds.append(
                remote(
                    src.at[0, rows, :],
                    x_in.at[leg * ROWS + h * BLOCK : leg * ROWS + (h + 1) * BLOCK, :],
                    feed_ss.at[h, leg],
                    feed_rs.at[h, leg],
                    to,
                )
            )
    for k in range(KVH):
        cols = slice(k * SPAN, (k + 1) * SPAN)
        for leg, (src, to) in enumerate(((cot_down, behind), (cot_up, ahead))):
            cots.append(
                remote(
                    src.at[0, :, cols],
                    g_in.at[leg * ROWS : (leg + 1) * ROWS, cols],
                    cot_ss.at[k, leg],
                    cot_rs.at[k, leg],
                    to,
                )
            )
    for leg, to in enumerate((behind, ahead)):
        earlies.append(
            remote(early_send.at[leg], early_recv.at[leg], early_ss.at[leg], early_rs.at[leg], to)
        )

    for copy in feeds:
        copy.start()
    early_cols = slice(EARLY * SPAN, (EARLY + 1) * SPAN)
    own = [
        pltpu.make_async_copy(src.at[0, :, early_cols], early_own.at[leg], local_sem.at[leg])
        for leg, src in enumerate((cot_down, cot_up))
    ]
    load_w = pltpu.make_async_copy(weight.at[0], w_buf, local_sem.at[2])
    for copy in own:
        copy.start()
    load_w.start()

    def group_sum(ref_tile):
        total = ref_tile(0).astype(F32)
        for j in range(1, GROUPS):
            total = total + ref_tile(j).astype(F32)
        return total

    for leg in range(2):
        own[leg].wait()
        early_send[leg] = group_sum(lambda j: early_own[leg, :, j * HD : (j + 1) * HD]).astype(BF16)
        earlies[leg].start()

    swap = [roster[0, leg, 0] == 1 for leg in range(2)]

    def normalize(h):
        for leg in range(2):

            @pl.loop(0, BLOCK // 16)
            def _(i):
                at = pl.ds(pl.multiple_of(leg * ROWS + h * BLOCK + i * 16, 16), 16)
                val = x_in[at, :].astype(F32)
                inv = lax.rsqrt(jnp.sum(val * val, axis=-1, keepdims=True) * (1.0 / D) + EPSILON)
                inverse[at, :] = jnp.broadcast_to(inv, (16, HD))
                normed[at, :] = (val * inv).astype(BF16)

    def set_grouped(k, leg, parts):
        first, second = parts
        cols = slice(k * HD, (k + 1) * HD)
        grouped[leg * ROWS : leg * ROWS + BLOCK, cols] = jnp.where(swap[leg], second, first).astype(BF16)
        grouped[leg * ROWS + BLOCK : (leg + 1) * ROWS, cols] = jnp.where(swap[leg], first, second).astype(BF16)

    def group(k):
        for leg in range(2):
            parts = []
            for b in range(2):
                lo = leg * ROWS + b * BLOCK
                parts.append(
                    group_sum(lambda j: g_in[lo : lo + BLOCK, k * SPAN + j * HD : k * SPAN + (j + 1) * HD])
                )
            set_grouped(k, leg, parts)

    def core_copy(k):
        return remote(core_send.at[k], core_recv.at[k], core_ss.at[k], core_rs.at[k], twin)

    def x_copy(k, j):
        return remote(
            x_send.at[k, j - 1], x_recv.at[k, j - 1], x_ss.at[k, j - 1], x_rs.at[k, j - 1], x_peer(j)
        )

    def y_copy(k, j):
        return remote(
            y_send.at[k, j - 1], y_recv.at[k, j - 1], y_ss.at[k, j - 1], y_rs.at[k, j - 1], y_peer(j)
        )

    half = NX * NY * HD
    step = 512

    def term(k):
        cols = slice(k * HD, (k + 1) * HD)

        @pl.loop(0, half // step)
        def _(i):
            at = pl.ds(pl.multiple_of(i * step, step), step)
            core_send[k, at, :] = jnp.dot(
                turned[1 - c, at, :], grouped[:, cols], preferred_element_type=F32
            ).astype(BF16)

        core_copy(k).start()

        @pl.loop(0, half // step)
        def _(i):
            at = pl.ds(pl.multiple_of(i * step, step), step)
            keep[k, at, :] = jnp.dot(turned[c, at, :], grouped[:, cols], preferred_element_type=F32)

    quarter = NY * HD

    def over_core(k):
        core_copy(k).wait_recv()
        for j in (2, 1, 3):
            at = pl.ds(pl.multiple_of(((x + j) % NX) * quarter, quarter), quarter)
            x_send[k, j - 1] = (keep[k, at, :] + core_recv[k, at, :].astype(F32)).astype(BF16)
            x_copy(k, j).start()
        at = pl.ds(pl.multiple_of(x * quarter, quarter), quarter)
        x_total[k] = keep[k, at, :] + core_recv[k, at, :].astype(F32)

    def over_x(k):
        for j in range(1, NX):
            x_copy(k, j).wait_recv()
        x_total[k] = (
            x_total[k] + x_recv[k, 0].astype(F32) + x_recv[k, 1].astype(F32) + x_recv[k, 2].astype(F32)
        )
        for j in range(1, NY):
            at = pl.ds(pl.multiple_of(((y + j) % NY) * HD, HD), HD)
            y_send[k, j - 1] = x_total[k, at, :].astype(BF16)
            y_copy(k, j).start()

    def over_y(k):
        for j in range(1, NY):
            y_copy(k, j).wait_recv()
        at = pl.ds(pl.multiple_of(y * HD, HD), HD)
        total = x_total[k, at, :]
        for j in range(1, NY):
            total = total + y_recv[k, j - 1].astype(F32)
        grad_buf[:, k * HD : (k + 1) * HD] = total * factor

    def send_next(k):
        for copy in cots[2 * k : 2 * k + 2]:
            copy.start()

    def sent(copies):
        for copy in copies:
            copy.wait_send()

    def received(copies):
        for copy in copies:
            copy.wait_recv()

    outs = []

    def write(src, dst, i):
        copy = pltpu.make_async_copy(src, dst, out_sem.at[i])
        copy.start()
        outs.append(copy)

    def finish_back(k):
        for leg in range(2):
            for b in range(2):
                lo = leg * ROWS + b * BLOCK
                other = leg * ROWS + (1 - b) * BLOCK

                @pl.loop(0, BLOCK // 16)
                def _(i):
                    at = pl.ds(pl.multiple_of(lo + i * 16, 16), 16)
                    at_other = pl.ds(pl.multiple_of(other + i * 16, 16), 16)
                    cols = slice(k * SPAN, (k + 1) * SPAN)
                    g = jnp.where(
                        swap[leg], g_in[at_other, cols].astype(F32), g_in[at, cols].astype(F32)
                    )
                    back_buf[at, cols] = (g + through[at, cols]).astype(BF16)

        cols = slice(k * SPAN, (k + 1) * SPAN)
        write(back_buf.at[0:ROWS, cols], back_down.at[0, :, cols], 2 * k)
        write(back_buf.at[ROWS:TOK, cols], back_up.at[0, :, cols], 2 * k + 1)

    sent(feeds[0:2])
    send_next(0)
    received(feeds[0:2])
    normalize(0)
    sent(feeds[2:4])
    send_next(1)
    received(feeds[2:4])
    normalize(1)

    @pl.loop(0, NX * NY * NC)
    def _(i):
        cols = pl.ds(pl.multiple_of(i * HD, HD), HD)
        to = pl.ds(pl.multiple_of((i // NC) * HD, HD), HD)
        turned[i % NC, to, :] = normed[:, cols].T

    received(earlies)
    for leg in range(2):
        set_grouped(
            EARLY, leg, [early_recv[leg, 0:BLOCK, :].astype(F32), early_recv[leg, BLOCK:ROWS, :].astype(F32)]
        )
    term(EARLY)

    load_w.wait()
    values[...] = jnp.zeros_like(values)

    @pl.loop(0, D // 512)
    def _(i):
        at = pl.ds(pl.multiple_of(i * 512, 512), 512)
        values[...] += jnp.dot(normed[:, at], w_buf[at, :], preferred_element_type=F32)

    over_core(EARLY)

    @pl.loop(0, TOK // 16)
    def _(i):
        at = pl.ds(pl.multiple_of(i * 16, 16), 16)
        for k in range(KVH):
            val = values[at, k * HD : (k + 1) * HD]
            for j in range(GROUPS):
                cols = slice((k * GROUPS + j) * HD, (k * GROUPS + j + 1) * HD)
                next_buf[at, cols] = (x_in[at, cols].astype(F32) + val).astype(BF16)

    write(next_buf.at[0:ROWS], next_down.at[0], 8)
    write(next_buf.at[ROWS:TOK], next_up.at[0], 9)

    sent(cots[0:2])
    send_next(2)
    received(cots[0:2])
    group(0)
    term(0)
    over_x(EARLY)
    over_core(0)

    sent(cots[2:4])
    send_next(3)
    received(cots[2:4])
    group(1)
    term(1)
    over_y(EARLY)
    over_x(0)
    over_core(1)

    received(cots[4:6])
    group(2)
    term(2)
    over_y(0)
    over_core(2)
    over_x(1)

    @pl.loop(0, D // 512)
    def _(i):
        at = pl.ds(pl.multiple_of(i * 512, 512), 512)
        through[:, at] = lax.dot_general(
            grouped[...], w_buf[at, :], (((1,), (1,)), ((), ())), preferred_element_type=F32
        )

    @pl.loop(0, TOK // 16)
    def _(i):
        at = pl.ds(pl.multiple_of(i * 16, 16), 16)
        inv = inverse[at, 0:1]
        scaled = x_in[at, :].astype(F32) * inv
        back_norm = through[at, :]
        mean = jnp.sum(back_norm * scaled, axis=-1, keepdims=True) * (1.0 / D)
        through[at, :] = inv * (back_norm - scaled * mean)

    over_x(2)
    for k in range(KVH):
        if k != EARLY:
            finish_back(k)
    over_y(1)
    over_y(2)
    write(grad_buf, grad.at[0], 10)

    received(cots[6:8])
    finish_back(EARLY)

    sent(cots[4:8])
    sent(earlies)
    for k in range(KVH):
        core_copy(k).wait_send()
        for j in range(1, NX):
            x_copy(k, j).wait_send()
        for j in range(1, NY):
            y_copy(k, j).wait_send()
    for copy in outs:
        copy.wait()


def on_device(feed_down, feed_up, cotangent_down, cotangent_up, roster, value_weight):
    factor = float(TOK * lax.axis_size("dp")) ** (-0.5)
    sem = pltpu.SemaphoreType.DMA
    half = NX * NY * HD
    return pl.pallas_call(
        lambda *refs: kernel(factor, *refs),
        out_shape=(
            *(jax.ShapeDtypeStruct((1, ROWS, D), BF16) for _ in range(4)),
            jax.ShapeDtypeStruct((1, D // (NX * NY * NC), KVH * HD), F32),
        ),
        in_specs=[pl.BlockSpec(memory_space=pl.ANY)] * 4
        + [pl.BlockSpec(memory_space=pltpu.SMEM), pl.BlockSpec(memory_space=pl.ANY)],
        out_specs=[pl.BlockSpec(memory_space=pl.ANY)] * 5,
        scratch_shapes=[
            pltpu.VMEM((TOK, D), BF16),
            pltpu.VMEM((TOK, D), BF16),
            pltpu.VMEM((2, ROWS, SPAN), BF16),
            pltpu.VMEM((2, ROWS, HD), BF16),
            pltpu.VMEM((2, ROWS, HD), BF16),
            pltpu.VMEM((D, KVH * HD), BF16),
            pltpu.VMEM((TOK, D), BF16),
            pltpu.VMEM((NC, half, TOK), BF16),
            pltpu.VMEM((TOK, HD), F32),
            pltpu.VMEM((TOK, KVH * HD), BF16),
            pltpu.VMEM((TOK, KVH * HD), F32),
            pltpu.VMEM((TOK, D), F32),
            pltpu.VMEM((TOK, D), BF16),
            pltpu.VMEM((TOK, D), BF16),
            pltpu.VMEM((KVH, half, HD), F32),
            pltpu.VMEM((KVH, half, HD), BF16),
            pltpu.VMEM((KVH, half, HD), BF16),
            pltpu.VMEM((KVH, NX - 1, NY * HD, HD), BF16),
            pltpu.VMEM((KVH, NX - 1, NY * HD, HD), BF16),
            pltpu.VMEM((KVH, NY * HD, HD), F32),
            pltpu.VMEM((KVH, NY - 1, HD, HD), BF16),
            pltpu.VMEM((KVH, NY - 1, HD, HD), BF16),
            pltpu.VMEM((HD, KVH * HD), F32),
            sem((2, 2)),
            sem((2, 2)),
            sem((KVH, 2)),
            sem((KVH, 2)),
            sem((2,)),
            sem((2,)),
            sem((KVH,)),
            sem((KVH,)),
            sem((KVH, NX - 1)),
            sem((KVH, NX - 1)),
            sem((KVH, NY - 1)),
            sem((KVH, NY - 1)),
            sem((3,)),
            sem((11,)),
        ],
        compiler_params=pltpu.CompilerParams(
            collective_id=0, has_side_effects=True, vmem_limit_bytes=56 * 1024 * 1024
        ),
        cost_estimate=pl.CostEstimate(flops=1_700_000_000, bytes_accessed=9_000_000, transcendentals=0),
    )(feed_down, feed_up, cotangent_down, cotangent_up, roster, value_weight)


def solution(mesh):
    placed = P("section", "dp", None)
    whole = P("section", None, None)
    return jax.shard_map(
        on_device,
        mesh=mesh,
        in_specs=(placed, placed, placed, placed, whole, whole),
        out_specs=(placed,) * 5,
        check_vma=False,
    )
```

```python
import jax
import jax.numpy as jnp
from jax import lax
from jax.experimental import pallas as pl
from jax.experimental.pallas import tpu as pltpu
from jax.sharding import PartitionSpec as P

MESH = pl.DeviceIdType.MESH
F32 = jnp.float32
BF16 = jnp.bfloat16

KVH = 4
HD = 128
GROUPS = 8
SPAN = GROUPS * HD
D = KVH * SPAN
NX, NY, NC = 4, 4, 2
ROWS = 64
BLOCK = 32
TOK = 2 * ROWS
EPSILON = 1e-05
PARTS = 2
WIDE = D // PARTS
HEADS = KVH // PARTS
AHEAD = tuple(range(KVH - HEADS, KVH))


def kernel(
    factor,
    feed_down,
    feed_up,
    cot_down,
    cot_up,
    roster,
    weight,
    next_down,
    next_up,
    back_down,
    back_up,
    grad,
    x_in,
    g_in,
    early_own,
    early_send,
    early_recv,
    w_buf,
    normed,
    turned,
    inverse,
    grouped,
    values,
    through,
    keep,
    core_send,
    core_recv,
    x_send,
    x_recv,
    x_total,
    y_send,
    y_recv,
    feed_ss,
    feed_rs,
    cot_ss,
    cot_rs,
    early_ss,
    early_rs,
    core_ss,
    core_rs,
    x_ss,
    x_rs,
    y_ss,
    y_rs,
    local_sem,
):
    sections = lax.axis_size("section")
    s = lax.axis_index("section")
    d = lax.axis_index("dp")
    x = d // (NY * NC)
    y = (d // NC) % NY
    c = d % NC
    onward, back = (next_down, next_up), (back_down, back_up)
    ahead = (lax.rem(s + 1, sections), d)
    behind = (lax.rem(s + sections - 1, sections), d)
    twin = (s, d + 1 - 2 * c)

    def x_peer(j):
        return (s, ((x + j) % NX) * (NY * NC) + y * NC + c)

    def y_peer(j):
        return (s, x * (NY * NC) + ((y + j) % NY) * NC + c)

    partners = [ahead, behind, twin]
    partners += [x_peer(j) for j in range(1, NX)]
    partners += [y_peer(j) for j in range(1, NY)]
    barrier = pltpu.get_barrier_semaphore()
    for partner in partners:
        pl.semaphore_signal(barrier, inc=1, device_id=partner, device_id_type=MESH)
    own = [
        pltpu.make_async_copy(
            src.at[0, :, AHEAD[0] * SPAN : (AHEAD[-1] + 1) * SPAN], early_own.at[leg], local_sem.at[leg]
        )
        for leg, src in enumerate((cot_down, cot_up))
    ]
    load_w = pltpu.make_async_copy(weight.at[0], w_buf, local_sem.at[2])
    for copy in own:
        copy.start()
    load_w.start()
    pl.semaphore_wait(barrier, len(partners))

    def remote(src, dst, ss, rs, to):
        return pltpu.make_async_remote_copy(
            src_ref=src, dst_ref=dst, send_sem=ss, recv_sem=rs, device_id=to, device_id_type=MESH
        )

    feeds, cots, earlies = [], [], []
    for h in range(2):
        rows = slice(h * BLOCK, (h + 1) * BLOCK)
        for leg, (src, to) in enumerate(((feed_down, ahead), (feed_up, behind))):
            feeds.append(
                remote(
                    src.at[0, rows, :],
                    x_in.at[leg * ROWS + h * BLOCK : leg * ROWS + (h + 1) * BLOCK, :],
                    feed_ss.at[h, leg],
                    feed_rs.at[h, leg],
                    to,
                )
            )
    for k in range(PARTS):
        cols = slice(k * WIDE, (k + 1) * WIDE)
        for leg, (src, to) in enumerate(((cot_down, behind), (cot_up, ahead))):
            cots.append(
                remote(
                    src.at[0, :, cols],
                    g_in.at[leg * ROWS : (leg + 1) * ROWS, cols],
                    cot_ss.at[k, leg],
                    cot_rs.at[k, leg],
                    to,
                )
            )
    for leg, to in enumerate((behind, ahead)):
        earlies.append(
            remote(early_send.at[leg], early_recv.at[leg], early_ss.at[leg], early_rs.at[leg], to)
        )

    for copy in feeds:
        copy.start()
    def group_sum(ref_tile):
        total = ref_tile(0).astype(F32)
        for j in range(1, GROUPS):
            total = total + ref_tile(j).astype(F32)
        return total

    for leg in range(2):
        own[leg].wait()
        for k in range(len(AHEAD)):
            early_send[leg, :, k * HD : (k + 1) * HD] = group_sum(
                lambda j: early_own[leg, :, k * SPAN + j * HD : k * SPAN + (j + 1) * HD]
            ).astype(BF16)
        earlies[leg].start()

    swap = [roster[0, leg, 0] == 1 for leg in range(2)]

    def normalize(h):
        for leg in range(2):

            @pl.loop(0, BLOCK // 16)
            def _(i):
                at = pl.ds(pl.multiple_of(leg * ROWS + h * BLOCK + i * 16, 16), 16)
                val = x_in[at, :].astype(F32)
                inv = lax.rsqrt(jnp.sum(val * val, axis=-1, keepdims=True) * (1.0 / D) + EPSILON)
                inverse[at, :] = jnp.broadcast_to(inv, (16, HD))
                normed[at, :] = (val * inv).astype(BF16)

    def set_grouped(leg, heads, first, second):
        cols = slice(heads[0] * HD, (heads[-1] + 1) * HD)
        grouped[leg * ROWS : leg * ROWS + BLOCK, cols] = jnp.where(swap[leg], second, first).astype(BF16)
        grouped[leg * ROWS + BLOCK : (leg + 1) * ROWS, cols] = jnp.where(swap[leg], first, second).astype(BF16)

    def group(k):
        for leg in range(2):
            parts = []
            for b in range(2):
                lo = leg * ROWS + b * BLOCK
                parts.append(
                    group_sum(lambda j: g_in[lo : lo + BLOCK, k * SPAN + j * HD : k * SPAN + (j + 1) * HD])
                )
            set_grouped(leg, (k,), *parts)

    def core_copy(k):
        return remote(core_send.at[k], core_recv.at[k], core_ss.at[k], core_rs.at[k], twin)

    def x_copy(k, j):
        return remote(
            x_send.at[k, j - 1], x_recv.at[k, j - 1], x_ss.at[k, j - 1], x_rs.at[k, j - 1], x_peer(j)
        )

    def y_copy(k, j):
        return remote(
            y_send.at[k, j - 1], y_recv.at[k, j - 1], y_ss.at[k, j - 1], y_rs.at[k, j - 1], y_peer(j)
        )

    half = NX * NY * HD
    step = 512

    def term(k):
        cols = slice(k * HD, (k + 1) * HD)

        @pl.loop(0, half // step)
        def _(i):
            at = pl.ds(pl.multiple_of(i * step, step), step)
            core_send[k, at, :] = jnp.dot(
                turned[1 - c, at, :], grouped[:, cols], preferred_element_type=F32
            ).astype(BF16)

        core_copy(k).start()

        @pl.loop(0, half // step)
        def _(i):
            at = pl.ds(pl.multiple_of(i * step, step), step)
            keep[k, at, :] = jnp.dot(turned[c, at, :], grouped[:, cols], preferred_element_type=F32)

    quarter = NY * HD

    def over_core(k):
        core_copy(k).wait_recv()
        for j in (2, 1, 3):
            at = pl.ds(pl.multiple_of(((x + j) % NX) * quarter, quarter), quarter)
            x_send[k, j - 1] = (keep[k, at, :] + core_recv[k, at, :].astype(F32)).astype(BF16)
            x_copy(k, j).start()
        at = pl.ds(pl.multiple_of(x * quarter, quarter), quarter)
        x_total[k] = keep[k, at, :] + core_recv[k, at, :].astype(F32)

    def over_x(k):
        for j in range(1, NX):
            x_copy(k, j).wait_recv()
        x_total[k] = (
            x_total[k] + x_recv[k, 0].astype(F32) + x_recv[k, 1].astype(F32) + x_recv[k, 2].astype(F32)
        )
        for j in range(1, NY):
            at = pl.ds(pl.multiple_of(((y + j) % NY) * HD, HD), HD)
            y_send[k, j - 1] = x_total[k, at, :].astype(BF16)
            y_copy(k, j).start()

    def over_y(k):
        for j in range(1, NY):
            y_copy(k, j).wait_recv()
        total = x_total[k, pl.ds(pl.multiple_of(y * HD, HD), HD), :]
        for j in range(1, NY):
            total = total + y_recv[k, j - 1].astype(F32)
        grad[:, k * HD : (k + 1) * HD] = total * factor

    def send_next(k):
        for copy in cots[2 * k : 2 * k + 2]:
            copy.start()

    def sent(copies):
        for copy in copies:
            copy.wait_send()

    def received(copies):
        for copy in copies:
            copy.wait_recv()

    def finish_back(k):
        for leg in range(2):
            for b in range(2):
                lo = leg * ROWS + b * BLOCK
                other = leg * ROWS + (1 - b) * BLOCK

                @pl.loop(0, BLOCK // 16)
                def _(i):
                    at = pl.ds(pl.multiple_of(lo + i * 16, 16), 16)
                    at_other = pl.ds(pl.multiple_of(other + i * 16, 16), 16)
                    cols = slice(k * SPAN, (k + 1) * SPAN)
                    g = jnp.where(
                        swap[leg], g_in[at_other, cols].astype(F32), g_in[at, cols].astype(F32)
                    )
                    to = pl.ds(pl.multiple_of(b * BLOCK + i * 16, 16), 16)
                    back[leg][to, cols] = (g + through[at, cols]).astype(BF16)

    sent(feeds)
    send_next(0)
    received(feeds)
    normalize(0)
    normalize(1)

    @pl.loop(0, NX * NY * NC)
    def _(i):
        cols = pl.ds(pl.multiple_of(i * HD, HD), HD)
        to = pl.ds(pl.multiple_of((i // NC) * HD, HD), HD)
        turned[i % NC, to, :] = normed[:, cols].T

    received(earlies)
    for leg in range(2):
        set_grouped(
            leg, AHEAD, early_recv[leg, 0:BLOCK, :].astype(F32), early_recv[leg, BLOCK:ROWS, :].astype(F32)
        )
    for k in AHEAD:
        term(k)
    for k in AHEAD:
        over_core(k)

    load_w.wait()
    values[...] = jnp.zeros_like(values)

    @pl.loop(0, D // 512)
    def _(i):
        at = pl.ds(pl.multiple_of(i * 512, 512), 512)
        values[...] += jnp.dot(normed[:, at], w_buf[at, :], preferred_element_type=F32)

    for leg in range(2):

        @pl.loop(0, ROWS // 16)
        def _(i):
            at = pl.ds(pl.multiple_of(leg * ROWS + i * 16, 16), 16)
            to = pl.ds(pl.multiple_of(i * 16, 16), 16)
            for k in range(KVH):
                val = values[at, k * HD : (k + 1) * HD]
                for j in range(GROUPS):
                    cols = slice((k * GROUPS + j) * HD, (k * GROUPS + j + 1) * HD)
                    onward[leg][to, cols] = (x_in[at, cols].astype(F32) + val).astype(BF16)

    for k in AHEAD:
        over_x(k)

    sent(cots[0:2])
    send_next(1)
    received(cots[0:2])
    for k in range(HEADS):
        group(k)
        term(k)
    for k in range(HEADS):
        over_core(k)

    @pl.loop(0, D // 512)
    def _(i):
        at = pl.ds(pl.multiple_of(i * 512, 512), 512)
        through[:, at] = lax.dot_general(
            grouped[...], w_buf[at, :], (((1,), (1,)), ((), ())), preferred_element_type=F32
        )

    @pl.loop(0, TOK // 16)
    def _(i):
        at = pl.ds(pl.multiple_of(i * 16, 16), 16)
        inv = inverse[at, 0:1]
        scaled = x_in[at, :].astype(F32) * inv
        back_norm = through[at, :]
        mean = jnp.sum(back_norm * scaled, axis=-1, keepdims=True) * (1.0 / D)
        through[at, :] = inv * (back_norm - scaled * mean)

    for k in range(HEADS):
        over_x(k)
    for k in range(HEADS):
        finish_back(k)

    received(cots[2:4])
    for k in AHEAD:
        finish_back(k)
    for k in (*AHEAD, *range(HEADS)):
        over_y(k)

    sent(cots[2:4])
    sent(earlies)
    for k in range(KVH):
        core_copy(k).wait_send()
        for j in range(1, NX):
            x_copy(k, j).wait_send()
        for j in range(1, NY):
            y_copy(k, j).wait_send()


def write_out(*refs):
    copies = [pltpu.make_async_copy(refs[i], refs[5 + i].at[0], refs[10].at[i]) for i in range(5)]
    for copy in copies:
        copy.start()
    for copy in copies:
        copy.wait()


def on_device(feed_down, feed_up, cotangent_down, cotangent_up, roster, value_weight):
    factor = float(TOK * lax.axis_size("dp")) ** (-0.5)
    sem = pltpu.SemaphoreType.DMA
    half = NX * NY * HD
    results = pl.pallas_call(
        lambda *refs: kernel(factor, *refs),
        out_shape=(
            *(pltpu.VMEM((ROWS, D), BF16) for _ in range(4)),
            pltpu.VMEM((HD, KVH * HD), F32),
        ),
        in_specs=[pl.BlockSpec(memory_space=pl.ANY)] * 4
        + [pl.BlockSpec(memory_space=pltpu.SMEM), pl.BlockSpec(memory_space=pl.ANY)],
        out_specs=[pl.BlockSpec(memory_space=pltpu.VMEM)] * 5,
        scratch_shapes=[
            pltpu.VMEM((TOK, D), BF16),
            pltpu.VMEM((TOK, D), BF16),
            pltpu.VMEM((2, ROWS, HEADS * SPAN), BF16),
            pltpu.VMEM((2, ROWS, HEADS * HD), BF16),
            pltpu.VMEM((2, ROWS, HEADS * HD), BF16),
            pltpu.VMEM((D, KVH * HD), BF16),
            pltpu.VMEM((TOK, D), BF16),
            pltpu.VMEM((NC, half, TOK), BF16),
            pltpu.VMEM((TOK, HD), F32),
            pltpu.VMEM((TOK, KVH * HD), BF16),
            pltpu.VMEM((TOK, KVH * HD), F32),
            pltpu.VMEM((TOK, D), F32),
            pltpu.VMEM((KVH, half, HD), F32),
            pltpu.VMEM((KVH, half, HD), BF16),
            pltpu.VMEM((KVH, half, HD), BF16),
            pltpu.VMEM((KVH, NX - 1, NY * HD, HD), BF16),
            pltpu.VMEM((KVH, NX - 1, NY * HD, HD), BF16),
            pltpu.VMEM((KVH, NY * HD, HD), F32),
            pltpu.VMEM((KVH, NY - 1, HD, HD), BF16),
            pltpu.VMEM((KVH, NY - 1, HD, HD), BF16),
            sem((2, 2)),
            sem((2, 2)),
            sem((PARTS, 2)),
            sem((PARTS, 2)),
            sem((2,)),
            sem((2,)),
            sem((KVH,)),
            sem((KVH,)),
            sem((KVH, NX - 1)),
            sem((KVH, NX - 1)),
            sem((KVH, NY - 1)),
            sem((KVH, NY - 1)),
            sem((3,)),
        ],
        compiler_params=pltpu.CompilerParams(
            collective_id=0, has_side_effects=True, vmem_limit_bytes=56 * 1024 * 1024
        ),
        cost_estimate=pl.CostEstimate(flops=1_700_000_000, bytes_accessed=9_000_000, transcendentals=0),
    )(feed_down, feed_up, cotangent_down, cotangent_up, roster, value_weight)
    results = [pltpu.with_memory_space_constraint(one, pltpu.VMEM) for one in results]
    return pl.pallas_call(
        write_out,
        out_shape=tuple(jax.ShapeDtypeStruct((1, *one.shape), one.dtype) for one in results),
        in_specs=[pl.BlockSpec(memory_space=pltpu.VMEM)] * 5,
        out_specs=[pl.BlockSpec(memory_space=pl.ANY)] * 5,
        scratch_shapes=[sem((5,))],
    )(*results)


def solution(mesh):
    placed = P("section", "dp", None)
    whole = P("section", None, None)
    return jax.shard_map(
        on_device,
        mesh=mesh,
        in_specs=(placed, placed, placed, placed, whole, whole),
        out_specs=(placed,) * 5,
        check_vma=False,
    )
```

```python
import jax
import jax.numpy as jnp
from jax import lax
from jax.experimental import pallas as pl
from jax.experimental.pallas import tpu as pltpu
from jax.sharding import PartitionSpec as P

MESH = pl.DeviceIdType.MESH
F32 = jnp.float32
BF16 = jnp.bfloat16

KVH = 4
HD = 128
GROUPS = 8
SPAN = GROUPS * HD
D = KVH * SPAN
NX, NY, NC = 4, 4, 2
ROWS = 64
BLOCK = 32
TOK = 2 * ROWS
EPSILON = 1e-05
CUTS = (0, SPAN, D)
PARTS = len(CUTS) - 1
AHEAD = tuple(range(1, KVH))


def kernel(
    factor,
    feed_down,
    feed_up,
    cot_down,
    cot_up,
    roster,
    weight,
    next_down,
    next_up,
    back_down,
    back_up,
    grad,
    x_in,
    g_in,
    early_own,
    early_send,
    early_recv,
    w_buf,
    normed,
    turned,
    inverse,
    grouped,
    values,
    through,
    keep,
    core_send,
    core_recv,
    x_send,
    x_recv,
    x_total,
    y_send,
    y_recv,
    feed_ss,
    feed_rs,
    cot_ss,
    cot_rs,
    early_ss,
    early_rs,
    core_ss,
    core_rs,
    x_ss,
    x_rs,
    y_ss,
    y_rs,
    local_sem,
    level_sem,
):
    sections = lax.axis_size("section")
    s = lax.axis_index("section")
    d = lax.axis_index("dp")
    x = d // (NY * NC)
    y = (d // NC) % NY
    c = d % NC
    onward, back = (next_down, next_up), (back_down, back_up)
    ahead = (lax.rem(s + 1, sections), d)
    behind = (lax.rem(s + sections - 1, sections), d)
    twin = (s, d + 1 - 2 * c)

    def x_peer(j):
        return (s, ((x + j) % NX) * (NY * NC) + y * NC + c)

    def y_peer(j):
        return (s, x * (NY * NC) + ((y + j) % NY) * NC + c)

    partners = [ahead, behind, twin]
    partners += [x_peer(j) for j in range(1, NX)]
    partners += [y_peer(j) for j in range(1, NY)]
    barrier = pltpu.get_barrier_semaphore()
    for partner in partners:
        pl.semaphore_signal(barrier, inc=1, device_id=partner, device_id_type=MESH)
    own = [
        pltpu.make_async_copy(
            src.at[0, :, AHEAD[0] * SPAN : (AHEAD[-1] + 1) * SPAN], early_own.at[leg], local_sem.at[leg]
        )
        for leg, src in enumerate((cot_down, cot_up))
    ]
    load_w = pltpu.make_async_copy(weight.at[0], w_buf, local_sem.at[2])
    for copy in own:
        copy.start()
    load_w.start()
    pl.semaphore_wait(barrier, len(partners))

    def remote(src, dst, ss, rs, to):
        return pltpu.make_async_remote_copy(
            src_ref=src, dst_ref=dst, send_sem=ss, recv_sem=rs, device_id=to, device_id_type=MESH
        )

    feeds, cots, earlies = [], [], []
    for h in range(2):
        rows = slice(h * BLOCK, (h + 1) * BLOCK)
        for leg, (src, to) in enumerate(((feed_down, ahead), (feed_up, behind))):
            feeds.append(
                remote(
                    src.at[0, rows, :],
                    x_in.at[leg * ROWS + h * BLOCK : leg * ROWS + (h + 1) * BLOCK, :],
                    feed_ss.at[h, leg],
                    feed_rs.at[h, leg],
                    to,
                )
            )
    for k in range(PARTS):
        cols = slice(CUTS[k], CUTS[k + 1])
        for leg, (src, to) in enumerate(((cot_down, behind), (cot_up, ahead))):
            cots.append(
                remote(
                    src.at[0, :, cols],
                    g_in.at[leg * ROWS : (leg + 1) * ROWS, cols],
                    cot_ss.at[k, leg],
                    cot_rs.at[k, leg],
                    to,
                )
            )
    for leg, to in enumerate((behind, ahead)):
        earlies.append(
            remote(early_send.at[leg], early_recv.at[leg], early_ss.at[leg], early_rs.at[leg], to)
        )

    for copy in feeds:
        copy.start()
    def group_sum(ref_tile):
        total = ref_tile(0).astype(F32)
        for j in range(1, GROUPS):
            total = total + ref_tile(j).astype(F32)
        return total

    for leg in range(2):
        own[leg].wait()
        for k in range(len(AHEAD)):
            early_send[leg, :, k * HD : (k + 1) * HD] = group_sum(
                lambda j: early_own[leg, :, k * SPAN + j * HD : k * SPAN + (j + 1) * HD]
            ).astype(BF16)
        earlies[leg].start()

    swap = [roster[0, leg, 0] == 1 for leg in range(2)]

    def normalize(h):
        for leg in range(2):

            @pl.loop(0, BLOCK // 16)
            def _(i):
                at = pl.ds(pl.multiple_of(leg * ROWS + h * BLOCK + i * 16, 16), 16)
                val = x_in[at, :].astype(F32)
                inv = lax.rsqrt(jnp.sum(val * val, axis=-1, keepdims=True) * (1.0 / D) + EPSILON)
                inverse[at, :] = jnp.broadcast_to(inv, (16, HD))
                normed[at, :] = (val * inv).astype(BF16)

    def set_grouped(leg, heads, first, second):
        cols = slice(heads[0] * HD, (heads[-1] + 1) * HD)
        grouped[leg * ROWS : leg * ROWS + BLOCK, cols] = jnp.where(swap[leg], second, first).astype(BF16)
        grouped[leg * ROWS + BLOCK : (leg + 1) * ROWS, cols] = jnp.where(swap[leg], first, second).astype(BF16)

    def group(k):
        for leg in range(2):
            parts = []
            for b in range(2):
                lo = leg * ROWS + b * BLOCK
                parts.append(
                    group_sum(lambda j: g_in[lo : lo + BLOCK, k * SPAN + j * HD : k * SPAN + (j + 1) * HD])
                )
            set_grouped(leg, (k,), *parts)

    def core_copy(k):
        return remote(core_send.at[k], core_recv.at[k], core_ss.at[k], core_rs.at[k], twin)

    def x_copy(k, j):
        return remote(
            x_send.at[k, j - 1], x_recv.at[k, j - 1], x_ss.at[k, j - 1], x_rs.at[k, j - 1], x_peer(j)
        )

    def y_copy(k, j):
        return remote(
            y_send.at[k, j - 1], y_recv.at[k, j - 1], y_ss.at[k, j - 1], y_rs.at[k, j - 1], y_peer(j)
        )

    half = NX * NY * HD
    step = 512

    def term(k):
        cols = slice(k * HD, (k + 1) * HD)

        @pl.loop(0, half // step)
        def _(i):
            at = pl.ds(pl.multiple_of(i * step, step), step)
            core_send[k, at, :] = jnp.dot(
                turned[1 - c, at, :], grouped[:, cols], preferred_element_type=F32
            ).astype(BF16)

        core_copy(k).start()

        @pl.loop(0, half // step)
        def _(i):
            at = pl.ds(pl.multiple_of(i * step, step), step)
            keep[k, at, :] = jnp.dot(turned[c, at, :], grouped[:, cols], preferred_element_type=F32)

    quarter = NY * HD

    def over_core(k):
        core_copy(k).wait_recv()
        for j in (2, 1, 3):
            at = pl.ds(pl.multiple_of(((x + j) % NX) * quarter, quarter), quarter)
            x_send[k, j - 1] = (keep[k, at, :] + core_recv[k, at, :].astype(F32)).astype(BF16)
            x_copy(k, j).start()
        at = pl.ds(pl.multiple_of(x * quarter, quarter), quarter)
        x_total[k] = keep[k, at, :] + core_recv[k, at, :].astype(F32)

    def over_x(k):
        for j in range(1, NX):
            x_copy(k, j).wait_recv()
        x_total[k] = (
            x_total[k] + x_recv[k, 0].astype(F32) + x_recv[k, 1].astype(F32) + x_recv[k, 2].astype(F32)
        )
        for j in range(1, NY):
            at = pl.ds(pl.multiple_of(((y + j) % NY) * HD, HD), HD)
            y_send[k, j - 1] = x_total[k, at, :].astype(BF16)
            y_copy(k, j).start()

    def over_y(k):
        for j in range(1, NY):
            y_copy(k, j).wait_recv()
        total = x_total[k, pl.ds(pl.multiple_of(y * HD, HD), HD), :]
        for j in range(1, NY):
            total = total + y_recv[k, j - 1].astype(F32)
        grad[:, k * HD : (k + 1) * HD] = total * factor

    def send_next(k):
        for copy in cots[2 * k : 2 * k + 2]:
            copy.start()

    def sent(copies):
        for copy in copies:
            copy.wait_send()

    def received(copies):
        for copy in copies:
            copy.wait_recv()

    def level(i):
        for j in range(1, NY):
            pl.semaphore_signal(level_sem.at[i], inc=1, device_id=y_peer(j), device_id_type=MESH)
        pl.semaphore_wait(level_sem.at[i], NY - 1)

    def finish_back(k):
        for leg in range(2):
            for b in range(2):
                lo = leg * ROWS + b * BLOCK
                other = leg * ROWS + (1 - b) * BLOCK

                @pl.loop(0, BLOCK // 16)
                def _(i):
                    at = pl.ds(pl.multiple_of(lo + i * 16, 16), 16)
                    at_other = pl.ds(pl.multiple_of(other + i * 16, 16), 16)
                    cols = slice(k * SPAN, (k + 1) * SPAN)
                    g = jnp.where(
                        swap[leg], g_in[at_other, cols].astype(F32), g_in[at, cols].astype(F32)
                    )
                    to = pl.ds(pl.multiple_of(b * BLOCK + i * 16, 16), 16)
                    back[leg][to, cols] = (g + through[at, cols]).astype(BF16)

    sent(feeds)
    level(0)
    send_next(0)
    received(feeds)
    normalize(0)
    normalize(1)

    @pl.loop(0, NX * NY * NC)
    def _(i):
        cols = pl.ds(pl.multiple_of(i * HD, HD), HD)
        to = pl.ds(pl.multiple_of((i // NC) * HD, HD), HD)
        turned[i % NC, to, :] = normed[:, cols].T

    received(earlies)
    for leg in range(2):
        set_grouped(
            leg, AHEAD, early_recv[leg, 0:BLOCK, :].astype(F32), early_recv[leg, BLOCK:ROWS, :].astype(F32)
        )
    for k in AHEAD:
        term(k)
    for k in AHEAD:
        over_core(k)
    sent(cots[0:2])
    send_next(1)

    load_w.wait()
    values[...] = jnp.zeros_like(values)

    @pl.loop(0, D // 512)
    def _(i):
        at = pl.ds(pl.multiple_of(i * 512, 512), 512)
        values[...] += jnp.dot(normed[:, at], w_buf[at, :], preferred_element_type=F32)

    for leg in range(2):

        @pl.loop(0, ROWS // 16)
        def _(i):
            at = pl.ds(pl.multiple_of(leg * ROWS + i * 16, 16), 16)
            to = pl.ds(pl.multiple_of(i * 16, 16), 16)
            for k in range(KVH):
                val = values[at, k * HD : (k + 1) * HD]
                for j in range(GROUPS):
                    cols = slice((k * GROUPS + j) * HD, (k * GROUPS + j + 1) * HD)
                    onward[leg][to, cols] = (x_in[at, cols].astype(F32) + val).astype(BF16)

    over_x(1)
    over_x(2)

    received(cots[0:2])
    group(0)
    term(0)
    over_x(3)
    over_core(0)

    @pl.loop(0, D // 512)
    def _(i):
        at = pl.ds(pl.multiple_of(i * 512, 512), 512)
        through[:, at] = lax.dot_general(
            grouped[...], w_buf[at, :], (((1,), (1,)), ((), ())), preferred_element_type=F32
        )

    @pl.loop(0, TOK // 16)
    def _(i):
        at = pl.ds(pl.multiple_of(i * 16, 16), 16)
        inv = inverse[at, 0:1]
        scaled = x_in[at, :].astype(F32) * inv
        back_norm = through[at, :]
        mean = jnp.sum(back_norm * scaled, axis=-1, keepdims=True) * (1.0 / D)
        through[at, :] = inv * (back_norm - scaled * mean)

    over_x(0)
    finish_back(0)

    received(cots[2:4])
    for k in AHEAD:
        finish_back(k)
    for k in (*AHEAD, 0):
        over_y(k)

    sent(cots[2:4])
    sent(earlies)
    for k in range(KVH):
        core_copy(k).wait_send()
        for j in range(1, NX):
            x_copy(k, j).wait_send()
        for j in range(1, NY):
            y_copy(k, j).wait_send()


def write_out(*refs):
    copies = [pltpu.make_async_copy(refs[i], refs[5 + i].at[0], refs[10].at[i]) for i in range(5)]
    for copy in copies:
        copy.start()
    for copy in copies:
        copy.wait()


def on_device(feed_down, feed_up, cotangent_down, cotangent_up, roster, value_weight):
    factor = float(TOK * lax.axis_size("dp")) ** (-0.5)
    sem = pltpu.SemaphoreType.DMA
    half = NX * NY * HD
    results = pl.pallas_call(
        lambda *refs: kernel(factor, *refs),
        out_shape=(
            *(pltpu.VMEM((ROWS, D), BF16) for _ in range(4)),
            pltpu.VMEM((HD, KVH * HD), F32),
        ),
        in_specs=[pl.BlockSpec(memory_space=pl.ANY)] * 4
        + [pl.BlockSpec(memory_space=pltpu.SMEM), pl.BlockSpec(memory_space=pl.ANY)],
        out_specs=[pl.BlockSpec(memory_space=pltpu.VMEM)] * 5,
        scratch_shapes=[
            pltpu.VMEM((TOK, D), BF16),
            pltpu.VMEM((TOK, D), BF16),
            pltpu.VMEM((2, ROWS, len(AHEAD) * SPAN), BF16),
            pltpu.VMEM((2, ROWS, len(AHEAD) * HD), BF16),
            pltpu.VMEM((2, ROWS, len(AHEAD) * HD), BF16),
            pltpu.VMEM((D, KVH * HD), BF16),
            pltpu.VMEM((TOK, D), BF16),
            pltpu.VMEM((NC, half, TOK), BF16),
            pltpu.VMEM((TOK, HD), F32),
            pltpu.VMEM((TOK, KVH * HD), BF16),
            pltpu.VMEM((TOK, KVH * HD), F32),
            pltpu.VMEM((TOK, D), F32),
            pltpu.VMEM((KVH, half, HD), F32),
            pltpu.VMEM((KVH, half, HD), BF16),
            pltpu.VMEM((KVH, half, HD), BF16),
            pltpu.VMEM((KVH, NX - 1, NY * HD, HD), BF16),
            pltpu.VMEM((KVH, NX - 1, NY * HD, HD), BF16),
            pltpu.VMEM((KVH, NY * HD, HD), F32),
            pltpu.VMEM((KVH, NY - 1, HD, HD), BF16),
            pltpu.VMEM((KVH, NY - 1, HD, HD), BF16),
            sem((2, 2)),
            sem((2, 2)),
            sem((PARTS, 2)),
            sem((PARTS, 2)),
            sem((2,)),
            sem((2,)),
            sem((KVH,)),
            sem((KVH,)),
            sem((KVH, NX - 1)),
            sem((KVH, NX - 1)),
            sem((KVH, NY - 1)),
            sem((KVH, NY - 1)),
            sem((3,)),
            pltpu.SemaphoreType.REGULAR((2,)),
        ],
        compiler_params=pltpu.CompilerParams(
            collective_id=0, has_side_effects=True, vmem_limit_bytes=56 * 1024 * 1024
        ),
        cost_estimate=pl.CostEstimate(flops=1_700_000_000, bytes_accessed=9_000_000, transcendentals=0),
    )(feed_down, feed_up, cotangent_down, cotangent_up, roster, value_weight)
    results = [pltpu.with_memory_space_constraint(one, pltpu.VMEM) for one in results]
    return pl.pallas_call(
        write_out,
        out_shape=tuple(jax.ShapeDtypeStruct((1, *one.shape), one.dtype) for one in results),
        in_specs=[pl.BlockSpec(memory_space=pltpu.VMEM)] * 5,
        out_specs=[pl.BlockSpec(memory_space=pl.ANY)] * 5,
        scratch_shapes=[sem((5,))],
    )(*results)


def solution(mesh):
    placed = P("section", "dp", None)
    whole = P("section", None, None)
    return jax.shard_map(
        on_device,
        mesh=mesh,
        in_specs=(placed, placed, placed, placed, whole, whole),
        out_specs=(placed,) * 5,
        check_vma=False,
    )
```

```python
import jax
import jax.numpy as jnp
from jax import lax
from jax.experimental import pallas as pl
from jax.experimental.pallas import tpu as pltpu
from jax.sharding import PartitionSpec as P

MESH = pl.DeviceIdType.MESH
F32 = jnp.float32
BF16 = jnp.bfloat16

KVH = 4
HD = 128
GROUPS = 8
SPAN = GROUPS * HD
D = KVH * SPAN
NX, NY, NC = 4, 4, 2
ROWS = 64
BLOCK = 32
TOK = 2 * ROWS
EPSILON = 1e-05
CUTS = (0, SPAN, D)
PARTS = len(CUTS) - 1
AHEAD = tuple(range(1, KVH))


def kernel(
    factor,
    feed_down,
    feed_up,
    cot_down,
    cot_up,
    roster,
    weight,
    next_down,
    next_up,
    back_down,
    back_up,
    grad,
    x_in,
    g_in,
    early_own,
    early_send,
    early_recv,
    w_buf,
    normed,
    turned,
    inverse,
    grouped,
    values,
    through,
    keep,
    core_send,
    core_recv,
    x_send,
    x_recv,
    x_total,
    y_send,
    y_recv,
    feed_ss,
    feed_rs,
    cot_ss,
    cot_rs,
    early_ss,
    early_rs,
    core_ss,
    core_rs,
    x_ss,
    x_rs,
    y_ss,
    y_rs,
    local_sem,
    level_sem,
):
    sections = lax.axis_size("section")
    s = lax.axis_index("section")
    d = lax.axis_index("dp")
    x = d // (NY * NC)
    y = (d // NC) % NY
    c = d % NC
    onward, back = (next_down, next_up), (back_down, back_up)
    ahead = (lax.rem(s + 1, sections), d)
    behind = (lax.rem(s + sections - 1, sections), d)
    twin = (s, d + 1 - 2 * c)

    def x_peer(j):
        return (s, ((x + j) % NX) * (NY * NC) + y * NC + c)

    def y_peer(j):
        return (s, x * (NY * NC) + ((y + j) % NY) * NC + c)

    partners = [ahead, behind, twin]
    partners += [x_peer(j) for j in range(1, NX)]
    partners += [y_peer(j) for j in range(1, NY)]
    barrier = pltpu.get_barrier_semaphore()
    for partner in partners:
        pl.semaphore_signal(barrier, inc=1, device_id=partner, device_id_type=MESH)
    own = [
        pltpu.make_async_copy(
            src.at[0, :, AHEAD[0] * SPAN : (AHEAD[-1] + 1) * SPAN], early_own.at[leg], local_sem.at[leg]
        )
        for leg, src in enumerate((cot_down, cot_up))
    ]
    load_w = pltpu.make_async_copy(weight.at[0], w_buf, local_sem.at[2])
    for copy in own:
        copy.start()
    load_w.start()
    pl.semaphore_wait(barrier, len(partners))

    def remote(src, dst, ss, rs, to):
        return pltpu.make_async_remote_copy(
            src_ref=src, dst_ref=dst, send_sem=ss, recv_sem=rs, device_id=to, device_id_type=MESH
        )

    feeds, cots, earlies = [], [], []
    for h in range(2):
        rows = slice(h * BLOCK, (h + 1) * BLOCK)
        for leg, (src, to) in enumerate(((feed_down, ahead), (feed_up, behind))):
            feeds.append(
                remote(
                    src.at[0, rows, :],
                    x_in.at[leg * ROWS + h * BLOCK : leg * ROWS + (h + 1) * BLOCK, :],
                    feed_ss.at[h, leg],
                    feed_rs.at[h, leg],
                    to,
                )
            )
    for k in range(PARTS):
        cols = slice(CUTS[k], CUTS[k + 1])
        for leg, (src, to) in enumerate(((cot_down, behind), (cot_up, ahead))):
            cots.append(
                remote(
                    src.at[0, :, cols],
                    g_in.at[leg * ROWS : (leg + 1) * ROWS, cols],
                    cot_ss.at[k, leg],
                    cot_rs.at[k, leg],
                    to,
                )
            )
    for leg, to in enumerate((behind, ahead)):
        earlies.append(
            remote(early_send.at[leg], early_recv.at[leg], early_ss.at[leg], early_rs.at[leg], to)
        )

    for copy in feeds:
        copy.start()
    def group_sum(ref_tile):
        total = ref_tile(0).astype(F32)
        for j in range(1, GROUPS):
            total = total + ref_tile(j).astype(F32)
        return total

    for leg in range(2):
        own[leg].wait()
        for k in range(len(AHEAD)):
            early_send[leg, :, k * HD : (k + 1) * HD] = group_sum(
                lambda j: early_own[leg, :, k * SPAN + j * HD : k * SPAN + (j + 1) * HD]
            ).astype(BF16)
        earlies[leg].start()

    swap = [roster[0, leg, 0] == 1 for leg in range(2)]

    def normalize(h):
        for leg in range(2):

            @pl.loop(0, BLOCK // 16)
            def _(i):
                at = pl.ds(pl.multiple_of(leg * ROWS + h * BLOCK + i * 16, 16), 16)
                val = x_in[at, :].astype(F32)
                inv = lax.rsqrt(jnp.sum(val * val, axis=-1, keepdims=True) * (1.0 / D) + EPSILON)
                inverse[at, :] = jnp.broadcast_to(inv, (16, HD))
                normed[at, :] = (val * inv).astype(BF16)

    def set_grouped(leg, heads, first, second):
        cols = slice(heads[0] * HD, (heads[-1] + 1) * HD)
        grouped[leg * ROWS : leg * ROWS + BLOCK, cols] = jnp.where(swap[leg], second, first).astype(BF16)
        grouped[leg * ROWS + BLOCK : (leg + 1) * ROWS, cols] = jnp.where(swap[leg], first, second).astype(BF16)

    def group(k):
        for leg in range(2):
            parts = []
            for b in range(2):
                lo = leg * ROWS + b * BLOCK
                parts.append(
                    group_sum(lambda j: g_in[lo : lo + BLOCK, k * SPAN + j * HD : k * SPAN + (j + 1) * HD])
                )
            set_grouped(leg, (k,), *parts)

    def core_copy(k):
        return remote(core_send.at[k], core_recv.at[k], core_ss.at[k], core_rs.at[k], twin)

    def x_copy(k, j):
        return remote(
            x_send.at[k, j - 1], x_recv.at[k, j - 1], x_ss.at[k, j - 1], x_rs.at[k, j - 1], x_peer(j)
        )

    def y_copy(k, j):
        return remote(
            y_send.at[k, j - 1], y_recv.at[k, j - 1], y_ss.at[k, j - 1], y_rs.at[k, j - 1], y_peer(j)
        )

    half = NX * NY * HD
    step = 512

    def term(k):
        cols = slice(k * HD, (k + 1) * HD)

        @pl.loop(0, half // step)
        def _(i):
            at = pl.ds(pl.multiple_of(i * step, step), step)
            core_send[k, at, :] = jnp.dot(
                turned[1 - c, at, :], grouped[:, cols], preferred_element_type=F32
            ).astype(BF16)

        core_copy(k).start()

        @pl.loop(0, half // step)
        def _(i):
            at = pl.ds(pl.multiple_of(i * step, step), step)
            keep[k, at, :] = jnp.dot(turned[c, at, :], grouped[:, cols], preferred_element_type=F32)

    quarter = NY * HD

    def over_core(k):
        core_copy(k).wait_recv()
        for j in (2, 1, 3):
            at = pl.ds(pl.multiple_of(((x + j) % NX) * quarter, quarter), quarter)
            x_send[k, j - 1] = (keep[k, at, :] + core_recv[k, at, :].astype(F32)).astype(BF16)
            x_copy(k, j).start()
        at = pl.ds(pl.multiple_of(x * quarter, quarter), quarter)
        x_total[k] = keep[k, at, :] + core_recv[k, at, :].astype(F32)

    def over_x(k):
        for j in range(1, NX):
            x_copy(k, j).wait_recv()
        x_total[k] = (
            x_total[k] + x_recv[k, 0].astype(F32) + x_recv[k, 1].astype(F32) + x_recv[k, 2].astype(F32)
        )
        for j in range(1, NY):
            at = pl.ds(pl.multiple_of(((y + j) % NY) * HD, HD), HD)
            y_send[k, j - 1] = x_total[k, at, :].astype(BF16)
            y_copy(k, j).start()

    def over_y(k):
        for j in range(1, NY):
            y_copy(k, j).wait_recv()
        total = x_total[k, pl.ds(pl.multiple_of(y * HD, HD), HD), :]
        for j in range(1, NY):
            total = total + y_recv[k, j - 1].astype(F32)
        grad[:, k * HD : (k + 1) * HD] = total * factor

    def send_next(k):
        for copy in cots[2 * k : 2 * k + 2]:
            copy.start()

    def sent(copies):
        for copy in copies:
            copy.wait_send()

    def received(copies):
        for copy in copies:
            copy.wait_recv()

    def level(i):
        for j in range(1, NY):
            pl.semaphore_signal(level_sem.at[i], inc=1, device_id=y_peer(j), device_id_type=MESH)
        pl.semaphore_wait(level_sem.at[i], NY - 1)

    def finish_back(k):
        for leg in range(2):
            for b in range(2):
                lo = leg * ROWS + b * BLOCK
                other = leg * ROWS + (1 - b) * BLOCK

                @pl.loop(0, BLOCK // 16)
                def _(i):
                    at = pl.ds(pl.multiple_of(lo + i * 16, 16), 16)
                    at_other = pl.ds(pl.multiple_of(other + i * 16, 16), 16)
                    cols = slice(k * SPAN, (k + 1) * SPAN)
                    g = jnp.where(
                        swap[leg], g_in[at_other, cols].astype(F32), g_in[at, cols].astype(F32)
                    )
                    to = pl.ds(pl.multiple_of(b * BLOCK + i * 16, 16), 16)
                    back[leg][to, cols] = (g + through[at, cols]).astype(BF16)

    sent(feeds)
    level(0)
    send_next(0)
    received(feeds)
    normalize(0)
    normalize(1)

    @pl.loop(0, NX * NY * NC)
    def _(i):
        cols = pl.ds(pl.multiple_of(i * HD, HD), HD)
        to = pl.ds(pl.multiple_of((i // NC) * HD, HD), HD)
        turned[i % NC, to, :] = normed[:, cols].T

    received(earlies)
    for leg in range(2):
        set_grouped(
            leg, AHEAD, early_recv[leg, 0:BLOCK, :].astype(F32), early_recv[leg, BLOCK:ROWS, :].astype(F32)
        )
    term(1)
    term(2)
    over_core(1)
    term(3)
    over_core(2)
    over_core(3)
    sent(cots[0:2])
    send_next(1)

    load_w.wait()
    values[...] = jnp.zeros_like(values)

    @pl.loop(0, D // 512)
    def _(i):
        at = pl.ds(pl.multiple_of(i * 512, 512), 512)
        values[...] += jnp.dot(normed[:, at], w_buf[at, :], preferred_element_type=F32)

    for leg in range(2):

        @pl.loop(0, ROWS // 16)
        def _(i):
            at = pl.ds(pl.multiple_of(leg * ROWS + i * 16, 16), 16)
            to = pl.ds(pl.multiple_of(i * 16, 16), 16)
            for k in range(KVH):
                val = values[at, k * HD : (k + 1) * HD]
                for j in range(GROUPS):
                    cols = slice((k * GROUPS + j) * HD, (k * GROUPS + j + 1) * HD)
                    onward[leg][to, cols] = (x_in[at, cols].astype(F32) + val).astype(BF16)

    over_x(1)
    over_x(2)

    received(cots[0:2])
    group(0)
    term(0)
    over_x(3)
    over_core(0)

    @pl.loop(0, D // 512)
    def _(i):
        at = pl.ds(pl.multiple_of(i * 512, 512), 512)
        through[:, at] = lax.dot_general(
            grouped[...], w_buf[at, :], (((1,), (1,)), ((), ())), preferred_element_type=F32
        )

    @pl.loop(0, TOK // 16)
    def _(i):
        at = pl.ds(pl.multiple_of(i * 16, 16), 16)
        inv = inverse[at, 0:1]
        scaled = x_in[at, :].astype(F32) * inv
        back_norm = through[at, :]
        mean = jnp.sum(back_norm * scaled, axis=-1, keepdims=True) * (1.0 / D)
        through[at, :] = inv * (back_norm - scaled * mean)

    over_x(0)
    finish_back(0)

    received(cots[2:4])
    for k in AHEAD:
        finish_back(k)
    for k in (*AHEAD, 0):
        over_y(k)

    sent(cots[2:4])
    sent(earlies)
    for k in range(KVH):
        core_copy(k).wait_send()
        for j in range(1, NX):
            x_copy(k, j).wait_send()
        for j in range(1, NY):
            y_copy(k, j).wait_send()


def write_out(*refs):
    copies = [pltpu.make_async_copy(refs[i], refs[5 + i].at[0], refs[10].at[i]) for i in range(5)]
    for copy in copies:
        copy.start()
    for copy in copies:
        copy.wait()


def on_device(feed_down, feed_up, cotangent_down, cotangent_up, roster, value_weight):
    factor = float(TOK * lax.axis_size("dp")) ** (-0.5)
    sem = pltpu.SemaphoreType.DMA
    half = NX * NY * HD
    results = pl.pallas_call(
        lambda *refs: kernel(factor, *refs),
        out_shape=(
            *(pltpu.VMEM((ROWS, D), BF16) for _ in range(4)),
            pltpu.VMEM((HD, KVH * HD), F32),
        ),
        in_specs=[pl.BlockSpec(memory_space=pl.ANY)] * 4
        + [pl.BlockSpec(memory_space=pltpu.SMEM), pl.BlockSpec(memory_space=pl.ANY)],
        out_specs=[pl.BlockSpec(memory_space=pltpu.VMEM)] * 5,
        scratch_shapes=[
            pltpu.VMEM((TOK, D), BF16),
            pltpu.VMEM((TOK, D), BF16),
            pltpu.VMEM((2, ROWS, len(AHEAD) * SPAN), BF16),
            pltpu.VMEM((2, ROWS, len(AHEAD) * HD), BF16),
            pltpu.VMEM((2, ROWS, len(AHEAD) * HD), BF16),
            pltpu.VMEM((D, KVH * HD), BF16),
            pltpu.VMEM((TOK, D), BF16),
            pltpu.VMEM((NC, half, TOK), BF16),
            pltpu.VMEM((TOK, HD), F32),
            pltpu.VMEM((TOK, KVH * HD), BF16),
            pltpu.VMEM((TOK, KVH * HD), F32),
            pltpu.VMEM((TOK, D), F32),
            pltpu.VMEM((KVH, half, HD), F32),
            pltpu.VMEM((KVH, half, HD), BF16),
            pltpu.VMEM((KVH, half, HD), BF16),
            pltpu.VMEM((KVH, NX - 1, NY * HD, HD), BF16),
            pltpu.VMEM((KVH, NX - 1, NY * HD, HD), BF16),
            pltpu.VMEM((KVH, NY * HD, HD), F32),
            pltpu.VMEM((KVH, NY - 1, HD, HD), BF16),
            pltpu.VMEM((KVH, NY - 1, HD, HD), BF16),
            sem((2, 2)),
            sem((2, 2)),
            sem((PARTS, 2)),
            sem((PARTS, 2)),
            sem((2,)),
            sem((2,)),
            sem((KVH,)),
            sem((KVH,)),
            sem((KVH, NX - 1)),
            sem((KVH, NX - 1)),
            sem((KVH, NY - 1)),
            sem((KVH, NY - 1)),
            sem((3,)),
            pltpu.SemaphoreType.REGULAR((2,)),
        ],
        compiler_params=pltpu.CompilerParams(
            collective_id=0, has_side_effects=True, vmem_limit_bytes=56 * 1024 * 1024
        ),
        cost_estimate=pl.CostEstimate(flops=1_700_000_000, bytes_accessed=9_000_000, transcendentals=0),
    )(feed_down, feed_up, cotangent_down, cotangent_up, roster, value_weight)
    results = [pltpu.with_memory_space_constraint(one, pltpu.VMEM) for one in results]
    return pl.pallas_call(
        write_out,
        out_shape=tuple(jax.ShapeDtypeStruct((1, *one.shape), one.dtype) for one in results),
        in_specs=[pl.BlockSpec(memory_space=pltpu.VMEM)] * 5,
        out_specs=[pl.BlockSpec(memory_space=pl.ANY)] * 5,
        scratch_shapes=[sem((5,))],
    )(*results)


def solution(mesh):
    placed = P("section", "dp", None)
    whole = P("section", None, None)
    return jax.shard_map(
        on_device,
        mesh=mesh,
        in_specs=(placed, placed, placed, placed, whole, whole),
        out_specs=(placed,) * 5,
        check_vma=False,
    )
```
